32 devices in a mesh: replica: 4 (over y, x), rollout: 8 (over z, core).
Axes of the slice: x: 2, y: 2, z: 4, core: 2. Of those that a mesh axis runs over, the one named last changes fastest.
Arguments:
- w_query: bfloat16 [8192, 8192], P('replica', 'rollout'), may hold values from -6 to 6
- gate_weight: bfloat16 [8192, 28672], P('replica', 'rollout'), may hold values from -6 to 6
- w_output: bfloat16 [8192, 8192], P('rollout', 'replica'), may hold values from -6 to 6
- input_state: float32 [3, 3, 8192, 64], P(None, None, 'rollout', 'replica'), may hold values from -3 to 3, as said below
- input_parts: float32 [4, 3, 8192, 64], P('replica', None, 'rollout'), may hold values from -6 to 6
- square_state: float32 [2, 3, 64, 8192], P(None, None, 'replica', 'rollout'), may hold values from -3 to 3, as said below
- square_parts: float32 [4, 2, 64, 8192], P('replica', None, None, 'rollout'), may hold values from -6 to 6
- gate_state: float32 [3, 64, 28672], P(None, 'replica', 'rollout'), may hold values from -3 to 3, as said below
- gate_parts: float32 [4, 64, 28672], P('replica', None, 'rollout'), may hold values from -6 to 6
Outputs:
- merged_query: bfloat16 [8192, 8192], P('replica', 'rollout')
- merged_gate: bfloat16 [8192, 28672], P('replica', 'rollout')
- merged_output: bfloat16 [8192, 8192], P('rollout', 'replica')
- new_input_state: float32 [3, 3, 8192, 64], P(None, None, 'rollout', 'replica')
- new_square_state: float32 [2, 3, 64, 8192], P(None, None, 'replica', 'rollout')
- new_gate_state: float32 [3, 64, 28672], P(None, 'replica', 'rollout')
The draws below stay inside these ranges and needn't reach their ends.
Inputs may be any that keep to these rules, and one draw needn't show every extreme that they name: `input_state`: along the dimension of size 3 the entries are the factor, its first moment and its second moment, the last one positive. `square_state`: along the dimension of size 3 the entries are the factor, its first moment and its second moment, the last one positive. `gate_state`: along the first dimension the entries are the factor, its first moment and its second moment, the last one positive.
All inputs are finite; a program needn't handle non-finite values.
Results may differ from the reference program's by a relative error of at most 0.0051.
Values may be sent and summed in bfloat16 or wider, within the bound.
A program may use at most 128 MiB of HBM per device.

```python
import jax
import jax.numpy as jnp
from jax import lax

D = 8192
FF = 28672
R = 64
STEP = 3
N_REPLICA = 4


def make_state(key, shape, stack_dim):
    keys = jax.random.split(key, 3)
    param = 0.125 * jnp.clip(jax.random.normal(keys[0], shape, jnp.float32), -6.0, 6.0)
    first = 0.5 * jnp.clip(jax.random.normal(keys[1], shape, jnp.float32), -6.0, 6.0)
    second = jnp.exp(jax.random.uniform(keys[2], shape, jnp.float32, jnp.log(0.0001), jnp.log(0.01)))
    return jnp.stack([param, first, second], axis=stack_dim)


def draw_input_state(key, part):
    return make_state(jax.random.fold_in(key, 11), (3, D, R), 1)


def draw_square_state(key, part):
    return make_state(jax.random.fold_in(key, 23), (2, R, D), 1)


def draw_gate_state(key, part):
    return make_state(jax.random.fold_in(key, 37), (R, FF), 0)


def raised(values, rng, source, target, parts, factor):
    owner, partner = [(jnp.arange(values.shape[axis_at]) // (values.shape[axis_at] // parts)).reshape([-1 if axis == axis_at else 1 for axis in range(values.ndim)]) for axis_at in (source, target)]
    chosen = jax.random.permutation(rng, parts)[partner]
    strong = (owner == chosen) | (owner == (partner + parts // 2) % parts)
    return jnp.where(strong, factor * values, values)


def block_scale(key, dims, shards, least, high):
    def one(dim, parts):
        steps = jax.random.uniform(jax.random.fold_in(jax.random.fold_in(key, 6), dim), (parts,), jnp.float32, least / len(shards), high / len(shards))
        return jnp.repeat(jnp.exp(steps), dims[dim] // parts).reshape((-1,) + (1,) * (len(dims) - dim - 1))

    gain = one(*shards[0])
    for cut in shards[1:]:
        gain = gain * one(*cut)
    return gain


def scatter_about(stream_key, shape, spread, most, shards=(), held_as=jnp.bfloat16):
    result = spread * jax.random.normal(stream_key, shape, jnp.float32)
    if shards:
        result = result * block_scale(stream_key, shape, shards, -0.22, 0.18)
    return jnp.clip(result, -most, most).astype(held_as)


def heavy_noise(own_key, extent, scale, limit, shards, heavy, held_as=jnp.bfloat16):
    drawn = scale * jax.random.normal(own_key, extent, jnp.float32)
    if shards:
        drawn = drawn * block_scale(own_key, extent, shards, -0.22, 0.18)
    return jnp.clip(raised(drawn, jax.random.fold_in(own_key, 3), *heavy), -limit, limit).astype(held_as)


def setup_inputs(seed: int = 0) -> dict:
    seeds = jax.random.split(jax.random.key(seed), 10)
    return {
        "w_query": scatter_about(seeds[0], (D, D), 1.0, 6.0, ((0, 4), (1, 8))),
        "gate_weight": scatter_about(seeds[1], (D, FF), 1.0, 6.0, ((0, 4), (1, 8))),
        "w_output": scatter_about(seeds[2], (D, D), 1.0, 6.0, ((0, 8), (1, 4))),
        "input_state": draw_input_state(jax.random.fold_in(seeds[9], 71), 0),
        "input_parts": heavy_noise(seeds[4], (N_REPLICA, 3, D, R), 1.0, 6.0, ((0, 4), (2, 8)), (0, 3, 4, 2.0), jnp.float32),
        "square_state": draw_square_state(jax.random.fold_in(seeds[9], 71), 0),
        "square_parts": heavy_noise(seeds[6], (N_REPLICA, 2, R, D), 1.0, 6.0, ((0, 4), (3, 8)), (0, 2, 4, 2.0), jnp.float32),
        "gate_state": draw_gate_state(jax.random.fold_in(seeds[9], 71), 0),
        "gate_parts": heavy_noise(seeds[8], (N_REPLICA, R, FF), 1.0, 6.0, ((0, 4), (2, 8)), (0, 1, 4, 2.0), jnp.float32),
    }


first_moment_decay = 0.9
beta_second = 0.999
learn_rate = 0.05
epsilon = 1e-08
adapter_scale = 2.0

def adam_update(param, first, second, grad):
    first_new = first_moment_decay * first + (1.0 - first_moment_decay) * grad
    second_new = beta_second * second + (1.0 - beta_second) * grad * grad
    fix_first = 1.0 - first_moment_decay ** STEP
    fix_second = 1.0 - beta_second ** STEP
    param_new = param - learn_rate * (first_new / fix_first) / (jnp.sqrt(second_new / fix_second) + epsilon)
    return (param_new, first_new, second_new)

def merge_weight(weight_matrix, left, right):
    weight_change = jnp.dot(left, right, preferred_element_type=jnp.float32)
    return (weight_matrix.astype(jnp.float32) + adapter_scale * weight_change).astype(jnp.bfloat16)

def reference(w_query, gate_weight, w_output, input_state, input_parts, square_state, square_parts, gate_state, gate_parts):
    input_grad = lax.optimization_barrier(jnp.sum(input_parts, axis=0))
    square_grad = lax.optimization_barrier(jnp.sum(square_parts, axis=0))
    gate_gradient = lax.optimization_barrier(jnp.sum(gate_parts, axis=0))
    new_input = jnp.stack(adam_update(input_state[:, 0], input_state[:, 1], input_state[:, 2], input_grad), axis=1)
    new_square = jnp.stack(adam_update(square_state[:, 0], square_state[:, 1], square_state[:, 2], square_grad), axis=1)
    updated_gate_weight = jnp.stack(adam_update(gate_state[0], gate_state[1], gate_state[2], gate_gradient), axis=0)
    input_factor = new_input[:, 0].astype(jnp.bfloat16)
    square_factor = new_square[:, 0].astype(jnp.bfloat16)
    gate_factor = updated_gate_weight[0].astype(jnp.bfloat16)
    merged_query = merge_weight(w_query, input_factor[0], square_factor[0])
    merged_gate = merge_weight(gate_weight, input_factor[1], gate_factor)
    merged_output = merge_weight(w_output, input_factor[2], square_factor[1])
    return (merged_query, merged_gate, merged_output, new_input, new_square, updated_gate_weight)
```

```python
import functools

import jax
import jax.numpy as jnp
from jax import lax
from jax.experimental import pallas as pl
from jax.experimental.pallas import tpu as pltpu
from jax.sharding import PartitionSpec as P

STEP = 3

first_moment_decay = 0.9
beta_second = 0.999
learn_rate = 0.05
epsilon = 1e-08
adapter_scale = 2.0

MESH = pl.DeviceIdType.MESH
BF16 = jnp.bfloat16
F32 = jnp.float32


def adam_update(param, first, second, grad):
    first_new = first_moment_decay * first + (1.0 - first_moment_decay) * grad
    second_new = beta_second * second + (1.0 - beta_second) * grad * grad
    fix_first = 1.0 - first_moment_decay**STEP
    fix_second = 1.0 - beta_second**STEP
    param_new = param - learn_rate * (first_new / fix_first) / (
        jnp.sqrt(second_new / fix_second) + epsilon
    )
    return (param_new, first_new, second_new)


def exchange_kernel(
    n, lines, width,
    in_parts, sq_parts, ga_parts, in_state, sq_state, ga_state, w_query, w_gate, w_out,
    slab, pair, gate, in_new, sq_new, ga_new, v_query, v_gate, v_out,
    in_raw, sq_raw, ga_raw, in_old, sq_old, ga_old,
    send0, send1, send2, recv0, recv1, recv2, line,
    load_sem, state_sem, weight_sem, rs_send, rs_recv, line_send, line_recv,
    swap_send, swap_recv, core_send, core_recv, ag_send, ag_recv,
):
    me = lax.axis_index("replica")
    spot = lax.axis_index("rollout")
    place, core = spot // 2, lax.rem(spot, 2)
    mate = place * 2 + (1 - core)
    rows = in_old.shape[2]

    pieces = (
        (
            (in_parts.at[0, 0], in_raw.at[0], 0, in_old.at[0], in_new.at[0]),
            (in_parts.at[0, 1], in_raw.at[1], width, in_old.at[1], in_new.at[1]),
            (sq_parts.at[0, 1], sq_raw.at[1], 2 * width, sq_old.at[1], sq_new.at[1]),
        ),
        (
            (in_parts.at[0, 2], in_raw.at[2], 0, in_old.at[2], in_new.at[2]),
            (sq_parts.at[0, 0], sq_raw.at[0], width, sq_old.at[0], sq_new.at[0]),
        ),
        ((ga_parts.at[0], ga_raw, 0, ga_old, ga_new),),
    )
    sends, recvs = (send0, send1, send2), (recv0, recv1, recv2)

    loads = []
    for group in pieces:
        for source, raw, *_ in group:
            loads.append(pltpu.make_async_copy(source, raw, load_sem.at[len(loads)]))
    states = [
        pltpu.make_async_copy(source, old, state_sem.at[i])
        for i, (source, old) in enumerate(
            ((in_state, in_old), (sq_state, sq_old), (ga_state, ga_old))
        )
    ]
    weights = [
        pltpu.make_async_copy(source, held, weight_sem.at[i])
        for i, (source, held) in enumerate(
            ((w_gate, v_gate), (w_query, v_query), (w_out, v_out))
        )
    ]
    for copy in loads + states + weights:
        copy.start()

    barrier = pltpu.get_barrier_semaphore()
    for d in range(1, n):
        pl.semaphore_signal(
            barrier, inc=1, device_id=(lax.rem(me + d, n), spot), device_id_type=MESH
        )
    for d in range(1, lines):
        pl.semaphore_signal(
            barrier, inc=1, device_id=(me, lax.rem(place + d, lines) * 2 + core), device_id_type=MESH
        )
    pl.semaphore_signal(barrier, inc=1, device_id=(me, mate), device_id_type=MESH)

    def scatter(g, d):
        peer = lax.rem(me + d, n)
        return pltpu.make_async_remote_copy(
            src_ref=sends[g].at[peer], dst_ref=recvs[g].at[d - 1],
            send_sem=rs_send.at[g, d - 1], recv_sem=rs_recv.at[g, d - 1],
            device_id=(peer, spot), device_id_type=MESH,
        )

    def along(d):
        return pltpu.make_async_remote_copy(
            src_ref=line.at[place], dst_ref=line.at[place],
            send_sem=line_send.at[d - 1], recv_sem=line_recv.at[d - 1],
            device_id=(me, lax.rem(place + d, lines) * 2 + core), device_id_type=MESH,
        )

    def swap(d, peer):
        return pltpu.make_async_remote_copy(
            src_ref=line.at[peer], dst_ref=slab.at[core, me],
            send_sem=swap_send.at[d], recv_sem=swap_recv.at[me],
            device_id=(peer, spot), device_id_type=MESH,
        )

    def across(owner):
        return pltpu.make_async_remote_copy(
            src_ref=slab.at[core, owner], dst_ref=slab.at[core, owner],
            send_sem=core_send.at[owner], recv_sem=core_recv.at[owner],
            device_id=(me, mate), device_id_type=MESH,
        )

    def gather(g, d):
        full = (pair, gate)[g]
        return pltpu.make_async_remote_copy(
            src_ref=full.at[me], dst_ref=full.at[me],
            send_sem=ag_send.at[g, d - 1], recv_sem=ag_recv.at[g, d - 1],
            device_id=(lax.rem(me + d, n), spot), device_id_type=MESH,
        )

    at_load = 0
    for g, group in enumerate(pieces):
        for _, raw, start, *_ in group:
            loads[at_load].wait()
            at_load += 1
            span = raw.shape[1]
            for j in range(n):
                sends[g][j, :, start : start + span] = raw[j * rows : (j + 1) * rows, :].astype(BF16)
        if g == 0:
            pl.semaphore_wait(barrier, n - 1 + lines - 1 + 1)
        for d in range(1, n):
            scatter(g, d).start()
    for copy in states:
        copy.wait()

    def update(g, factor):
        for d in range(1, n):
            scatter(g, d).wait_recv()
        mine = pl.ds(pl.multiple_of(me * rows, rows), rows)
        for _, raw, start, old, new in pieces[g]:
            span = raw.shape[1]
            step = 512 if span % 512 == 0 else 256
            for c in range(0, span, step):
                here, there = slice(c, c + step), slice(start + c, start + c + step)
                grad = raw[mine, here]
                for d in range(1, n):
                    grad = grad + recvs[g][d - 1, :, there].astype(F32)
                param, first, second = adam_update(old[0, :, here], old[1, :, here], old[2, :, here], grad)
                new[0, :, here] = param
                new[1, :, here] = first
                new[2, :, here] = second
                factor[:, there] = param.astype(BF16)

    def pass_on(d):
        if d:
            along_from = lax.rem(place + lines - d, lines)
            pltpu.make_async_remote_copy(
                src_ref=line.at[along_from], dst_ref=line.at[along_from],
                send_sem=line_send.at[d - 1], recv_sem=line_recv.at[d - 1],
                device_id=(me, lax.rem(place + d, lines) * 2 + core), device_id_type=MESH,
            ).wait_recv()
        peer = lax.rem(place + lines - d, lines)

        @pl.when(peer != me)
        def _():
            swap(d, peer).start()

        @pl.when(peer == me)
        def _():
            slab[core, me] = line[me]

    update(0, line.at[place])
    for d in range(1, lines):
        along(d).start()
    pass_on(0)
    update(1, pair.at[me])
    for d in range(1, n):
        gather(0, d).start()
    pass_on(1)
    update(2, gate.at[me])
    for d in range(1, n):
        gather(1, d).start()
    for d in range(2, lines):
        pass_on(d)

    across(me).start()
    for d in range(1, n):
        owner = lax.rem(me + d, n)
        pltpu.make_async_remote_copy(
            src_ref=line.at[me], dst_ref=slab.at[core, owner],
            send_sem=swap_send.at[d], recv_sem=swap_recv.at[owner],
            device_id=(owner, spot), device_id_type=MESH,
        ).wait_recv()
        across(owner).start()

    for copy in weights:
        copy.wait()
    for g in range(3):
        for d in range(1, n):
            scatter(g, d).wait_send()
    for d in range(1, lines):
        along(d).wait_send()
    for d in range(lines):
        peer = lax.rem(place + lines - d, lines)

        @pl.when(peer != me)
        def _():
            swap(d, peer).wait_send()

    for g, full in enumerate((pair, gate)):
        for d in range(1, n):
            gather(g, d).wait_send()
            owner = lax.rem(me + n - d, n)
            pltpu.make_async_remote_copy(
                src_ref=full.at[owner], dst_ref=full.at[owner],
                send_sem=ag_send.at[g, d - 1], recv_sem=ag_recv.at[g, d - 1],
                device_id=(lax.rem(me + d, n), spot), device_id_type=MESH,
            ).wait_recv()
    for d in range(n):
        owner = lax.rem(me + d, n)
        across(owner).wait_send()
        pltpu.make_async_remote_copy(
            src_ref=slab.at[1 - core, owner], dst_ref=slab.at[1 - core, owner],
            send_sem=core_send.at[owner], recv_sem=core_recv.at[owner],
            device_id=(me, mate), device_id_type=MESH,
        ).wait_recv()


def merge_kernel(
    width,
    slab, pair, gate, in_new, sq_new, ga_new, v_query, v_gate, v_out,
    m_query, m_gate, m_out, in_out, sq_out, ga_out,
    s_query, s_gate, s_out, state_sem, sem,
):
    n, rows = slab.shape[1], slab.shape[2]
    rank = n * rows

    states = [
        pltpu.make_async_copy(new, out, state_sem.at[i])
        for i, (new, out) in enumerate(((in_new, in_out), (sq_new, sq_out), (ga_new, ga_out)))
    ]
    for copy in states:
        copy.start()

    def flat(block):
        if rows % 16 == 0:
            return block.reshape(rank, block.shape[-1])
        return block.astype(F32).reshape(rank, block.shape[-1]).astype(BF16)

    def merge(which, held, staged, merged, left, rights, first, count):
        slots, tile = staged.shape[:2]
        done = first // tile

        def out_copy(i):
            slot = lax.rem(i, slots)
            at = pl.ds(pl.multiple_of(i * tile, tile), tile)
            return pltpu.make_async_copy(staged.at[slot], merged.at[at], sem.at[which, slot])

        def body(i, _):
            whole = done + i
            slot = lax.rem(whole, slots)

            @pl.when(whole >= slots)
            def _():
                out_copy(whole - slots).wait()

            at = pl.ds(pl.multiple_of(whole * tile, tile), tile)
            lhs = left(pl.ds(pl.multiple_of(i * tile, tile), tile)) * adapter_scale
            for start, span, right in rights:
                step = 512 if span % 512 == 0 else 256
                for c in range(0, span, step):
                    change = lax.dot_general(
                        lhs, right(slice(c, c + step)), (((0,), (0,)), ((), ())),
                        preferred_element_type=F32,
                    )
                    there = slice(start + c, start + c + step)
                    staged[slot, :, there] = (held[at, there].astype(F32) + change).astype(BF16)
            out_copy(whole).start()
            return 0

        lax.fori_loop(0, count // tile, body, 0)

    def drain(which, staged, merged):
        slots, tile = staged.shape[:2]
        steps = merged.shape[0] // tile
        for i in range(max(0, steps - slots), steps):
            pltpu.make_async_copy(
                staged.at[i % slots], merged.at[i * tile : (i + 1) * tile], sem.at[which, i % slots]
            ).wait()

    def slab_left(j, start):
        return lambda at: flat(slab[j, :, :, pl.ds(start + at.start, at.size)])

    hidden = gate.shape[2]
    for j in range(2):
        merge(
            0, v_gate, s_gate, m_gate, slab_left(j, width),
            ((0, hidden, lambda at: flat(gate[:, :, at])),), j * width, width,
        )
    for j in range(2):
        merge(
            1, v_query, s_query, m_query, slab_left(j, 0),
            ((0, width, lambda at: flat(pair[:, :, width + at.start : width + at.stop])),),
            j * width, width,
        )

    def out_right(j):
        return lambda at: flat(slab[j, :, :, 2 * width + at.start : 2 * width + at.stop])

    merge(
        2, v_out, s_out, m_out, lambda at: flat(pair[:, :, at]),
        ((0, width, out_right(0)), (width, width, out_right(1))), 0, width,
    )
    for which, (staged, merged) in enumerate(((s_gate, m_gate), (s_query, m_query), (s_out, m_out))):
        drain(which, staged, merged)
    for copy in states:
        copy.wait()


def on_device(
    n, lines,
    w_query, gate_weight, w_output, input_state, input_parts,
    square_state, square_parts, gate_state, gate_parts,
):
    in_state, in_parts = jnp.swapaxes(input_state, 2, 3), jnp.swapaxes(input_parts, 2, 3)
    rank, width = in_parts.shape[2:]
    rows = in_state.shape[2]
    hidden = gate_parts.shape[2]
    spans = (3 * width, 2 * width, hidden)
    dma = pltpu.SemaphoreType.DMA
    hbm = pl.BlockSpec(memory_space=pltpu.HBM)
    vmem = pl.BlockSpec(memory_space=pltpu.VMEM)

    held = pl.pallas_call(
        functools.partial(exchange_kernel, n, lines, width),
        out_shape=[
            pltpu.VMEM((2, n, rows, 3 * width), BF16),
            pltpu.VMEM((n, rows, 2 * width), BF16),
            pltpu.VMEM((n, rows, hidden), BF16),
            pltpu.VMEM(in_state.shape, F32),
            pltpu.VMEM(square_state.shape, F32),
            pltpu.VMEM(gate_state.shape, F32),
            pltpu.VMEM(w_query.shape, BF16),
            pltpu.VMEM(gate_weight.shape, BF16),
            pltpu.VMEM(w_output.shape, BF16),
        ],
        in_specs=[hbm] * 9,
        out_specs=[vmem] * 9,
        scratch_shapes=[
            pltpu.VMEM(in_parts.shape[1:], F32),
            pltpu.VMEM(square_parts.shape[1:], F32),
            pltpu.VMEM(gate_parts.shape[1:], F32),
            pltpu.VMEM(in_state.shape, F32),
            pltpu.VMEM(square_state.shape, F32),
            pltpu.VMEM(gate_state.shape, F32),
            *(pltpu.VMEM((n, rows, span), BF16) for span in spans),
            *(pltpu.VMEM((n - 1, rows, span), BF16) for span in spans),
            pltpu.VMEM((lines, rows, 3 * width), BF16),
            dma((6,)), dma((3,)), dma((3,)),
            dma((3, n - 1)), dma((3, n - 1)),
            dma((lines - 1,)), dma((lines - 1,)),
            dma((lines,)), dma((n,)),
            dma((n,)), dma((n,)),
            dma((2, n - 1)), dma((2, n - 1)),
        ],
        compiler_params=pltpu.CompilerParams(
            collective_id=0, has_side_effects=True, vmem_limit_bytes=16 * 2**20
        ),
        name="exchange",
    )(
        *(
            pltpu.with_memory_space_constraint(x, pltpu.HBM)
            for x in (
                in_parts, square_parts, gate_parts, in_state, square_state, gate_state,
                w_query, gate_weight, w_output,
            )
        )
    )
    merged_query, merged_gate, merged_output, new_input, new_square, new_gate = pl.pallas_call(
        functools.partial(merge_kernel, width),
        out_shape=[
            jax.ShapeDtypeStruct(w_query.shape, BF16),
            jax.ShapeDtypeStruct(gate_weight.shape, BF16),
            jax.ShapeDtypeStruct(w_output.shape, BF16),
            jax.ShapeDtypeStruct(in_state.shape, F32),
            jax.ShapeDtypeStruct(square_state.shape, F32),
            jax.ShapeDtypeStruct(gate_state.shape, F32),
        ],
        in_specs=[vmem] * 9,
        out_specs=[hbm] * 6,
        scratch_shapes=[
            *(pltpu.VMEM((4, 128, w.shape[1]), BF16) for w in (w_query, gate_weight, w_output)),
            dma((3,)),
            dma((3, 4)),
        ],
        compiler_params=pltpu.CompilerParams(vmem_limit_bytes=16 * 2**20),
        name="merge",
    )(*(pltpu.with_memory_space_constraint(x, pltpu.VMEM) for x in held))
    return (merged_query, merged_gate, merged_output, jnp.swapaxes(new_input, 2, 3), new_square, new_gate)


def solution(mesh):
    n, lines = mesh.shape["replica"], mesh.shape["rollout"] // 2
    assert n == lines
    return jax.shard_map(
        functools.partial(on_device, n, lines),
        mesh=mesh,
        in_specs=(
            P("replica", "rollout"),
            P("replica", "rollout"),
            P("rollout", "replica"),
            P(None, None, "rollout", "replica"),
            P("replica", None, "rollout", None),
            P(None, None, "replica", "rollout"),
            P("replica", None, None, "rollout"),
            P(None, "replica", "rollout"),
            P("replica", None, "rollout"),
        ),
        out_specs=(
            P("replica", "rollout"),
            P("replica", "rollout"),
            P("rollout", "replica"),
            P(None, None, "rollout", "replica"),
            P(None, None, "replica", "rollout"),
            P(None, "replica", "rollout"),
        ),
        check_vma=False,
    )
```

```python
import functools

import jax
import jax.numpy as jnp
from jax import lax
from jax.experimental import pallas as pl
from jax.experimental.pallas import tpu as pltpu
from jax.sharding import PartitionSpec as P

STEP = 3

first_moment_decay = 0.9
beta_second = 0.999
learn_rate = 0.05
epsilon = 1e-08
adapter_scale = 2.0

MESH = pl.DeviceIdType.MESH
BF16 = jnp.bfloat16
F32 = jnp.float32


def adam_update(param, first, second, grad):
    first_new = first_moment_decay * first + (1.0 - first_moment_decay) * grad
    second_new = beta_second * second + (1.0 - beta_second) * grad * grad
    fix_first = 1.0 - first_moment_decay**STEP
    fix_second = 1.0 - beta_second**STEP
    param_new = param - learn_rate * (first_new / fix_first) / (
        jnp.sqrt(second_new / fix_second) + epsilon
    )
    return (param_new, first_new, second_new)


def exchange_kernel(
    n, lines, width,
    in_parts, sq_parts, ga_parts, in_state, sq_state, ga_state, w_query, w_gate, w_out,
    slab, pair, gate, in_new, sq_new, ga_new, v_query, v_gate, v_out,
    in_raw, sq_raw, ga_raw, in_old, sq_old, ga_old,
    send0, send1, send2, recv0, recv1, recv2, line,
    load_sem, state_sem, weight_sem, rs_send, rs_recv, line_send, line_recv,
    swap_send, swap_recv, core_send, core_recv, ag_send, ag_recv,
):
    me = lax.axis_index("replica")
    spot = lax.axis_index("rollout")
    place, core = spot // 2, lax.rem(spot, 2)
    mate = place * 2 + (1 - core)
    rows = in_old.shape[2]

    pieces = (
        (
            (in_parts.at[0, 0], in_raw.at[0], 0, in_old.at[0], in_new.at[0]),
            (in_parts.at[0, 1], in_raw.at[1], width, in_old.at[1], in_new.at[1]),
            (sq_parts.at[0, 1], sq_raw.at[1], 2 * width, sq_old.at[1], sq_new.at[1]),
        ),
        (
            (in_parts.at[0, 2], in_raw.at[2], 0, in_old.at[2], in_new.at[2]),
            (sq_parts.at[0, 0], sq_raw.at[0], width, sq_old.at[0], sq_new.at[0]),
        ),
        ((ga_parts.at[0], ga_raw, 0, ga_old, ga_new),),
    )
    sends, recvs = (send0, send1, send2), (recv0, recv1, recv2)

    loads = []
    for group in pieces:
        for source, raw, *_ in group:
            loads.append(pltpu.make_async_copy(source, raw, load_sem.at[len(loads)]))
    states = [
        pltpu.make_async_copy(source, old, state_sem.at[i])
        for i, (source, old) in enumerate(
            ((in_state, in_old), (sq_state, sq_old), (ga_state, ga_old))
        )
    ]
    weights = [
        pltpu.make_async_copy(source, held, weight_sem.at[i])
        for i, (source, held) in enumerate(
            ((w_gate, v_gate), (w_query, v_query), (w_out, v_out))
        )
    ]
    for copy in loads + states + weights:
        copy.start()

    barrier = pltpu.get_barrier_semaphore()
    for d in range(1, n):
        pl.semaphore_signal(
            barrier, inc=1, device_id=(lax.rem(me + d, n), spot), device_id_type=MESH
        )
    for d in range(1, lines):
        pl.semaphore_signal(
            barrier, inc=1, device_id=(me, lax.rem(place + d, lines) * 2 + core), device_id_type=MESH
        )
    pl.semaphore_signal(barrier, inc=1, device_id=(me, mate), device_id_type=MESH)

    def scatter(g, d):
        peer = lax.rem(me + d, n)
        return pltpu.make_async_remote_copy(
            src_ref=sends[g].at[peer], dst_ref=recvs[g].at[d - 1],
            send_sem=rs_send.at[g, d - 1], recv_sem=rs_recv.at[g, d - 1],
            device_id=(peer, spot), device_id_type=MESH,
        )

    def along(d):
        return pltpu.make_async_remote_copy(
            src_ref=line.at[place], dst_ref=line.at[place],
            send_sem=line_send.at[d - 1], recv_sem=line_recv.at[d - 1],
            device_id=(me, lax.rem(place + d, lines) * 2 + core), device_id_type=MESH,
        )

    def swap(d, peer):
        return pltpu.make_async_remote_copy(
            src_ref=line.at[peer], dst_ref=slab.at[core, me],
            send_sem=swap_send.at[d], recv_sem=swap_recv.at[me],
            device_id=(peer, spot), device_id_type=MESH,
        )

    def across(owner):
        return pltpu.make_async_remote_copy(
            src_ref=slab.at[core, owner], dst_ref=slab.at[core, owner],
            send_sem=core_send.at[owner], recv_sem=core_recv.at[owner],
            device_id=(me, mate), device_id_type=MESH,
        )

    def gather(g, d):
        full = (pair, gate)[g]
        return pltpu.make_async_remote_copy(
            src_ref=full.at[me], dst_ref=full.at[me],
            send_sem=ag_send.at[g, d - 1], recv_sem=ag_recv.at[g, d - 1],
            device_id=(lax.rem(me + d, n), spot), device_id_type=MESH,
        )

    at_load = 0
    for g, group in enumerate(pieces):
        for _, raw, start, *_ in group:
            loads[at_load].wait()
            at_load += 1
            span = raw.shape[1]
            for j in range(n):
                sends[g][j, :, start : start + span] = raw[j * rows : (j + 1) * rows, :].astype(BF16)
        if g == 0:
            pl.semaphore_wait(barrier, n - 1 + lines - 1 + 1)
        for d in range(1, n):
            scatter(g, d).start()
    for copy in states:
        copy.wait()

    def update(g, factor):
        for d in range(1, n):
            scatter(g, d).wait_recv()
        mine = pl.ds(pl.multiple_of(me * rows, rows), rows)
        for _, raw, start, old, new in pieces[g]:
            span = raw.shape[1]
            step = 512 if span % 512 == 0 else 256
            for c in range(0, span, step):
                here, there = slice(c, c + step), slice(start + c, start + c + step)
                grad = raw[mine, here]
                for d in range(1, n):
                    grad = grad + recvs[g][d - 1, :, there].astype(F32)
                param, first, second = adam_update(old[0, :, here], old[1, :, here], old[2, :, here], grad)
                new[0, :, here] = param
                new[1, :, here] = first
                new[2, :, here] = second
                factor[:, there] = param.astype(BF16)

    def pass_on(d):
        if d:
            along_from = lax.rem(place + lines - d, lines)
            pltpu.make_async_remote_copy(
                src_ref=line.at[along_from], dst_ref=line.at[along_from],
                send_sem=line_send.at[d - 1], recv_sem=line_recv.at[d - 1],
                device_id=(me, lax.rem(place + d, lines) * 2 + core), device_id_type=MESH,
            ).wait_recv()
        peer = lax.rem(place + lines - d, lines)

        @pl.when(peer != me)
        def _():
            swap(d, peer).start()

        @pl.when(peer == me)
        def _():
            slab[core, me] = line[me]

    update(0, line.at[place])
    for d in range(1, lines):
        along(d).start()
    pass_on(0)
    update(1, pair.at[me])
    for d in range(1, n):
        gather(0, d).start()
    pass_on(1)
    update(2, gate.at[me])
    for d in range(1, n):
        gather(1, d).start()
    for d in range(2, lines):
        pass_on(d)

    across(me).start()
    for d in range(1, n):
        owner = lax.rem(me + d, n)
        pltpu.make_async_remote_copy(
            src_ref=line.at[me], dst_ref=slab.at[core, owner],
            send_sem=swap_send.at[d], recv_sem=swap_recv.at[owner],
            device_id=(owner, spot), device_id_type=MESH,
        ).wait_recv()
        across(owner).start()

    for copy in weights:
        copy.wait()
    for g in range(3):
        for d in range(1, n):
            scatter(g, d).wait_send()
    for d in range(1, lines):
        along(d).wait_send()
    for d in range(lines):
        peer = lax.rem(place + lines - d, lines)

        @pl.when(peer != me)
        def _():
            swap(d, peer).wait_send()

    for g, full in enumerate((pair, gate)):
        for d in range(1, n):
            gather(g, d).wait_send()
            owner = lax.rem(me + n - d, n)
            pltpu.make_async_remote_copy(
                src_ref=full.at[owner], dst_ref=full.at[owner],
                send_sem=ag_send.at[g, d - 1], recv_sem=ag_recv.at[g, d - 1],
                device_id=(lax.rem(me + d, n), spot), device_id_type=MESH,
            ).wait_recv()
    for d in range(n):
        owner = lax.rem(me + d, n)
        across(owner).wait_send()
        pltpu.make_async_remote_copy(
            src_ref=slab.at[1 - core, owner], dst_ref=slab.at[1 - core, owner],
            send_sem=core_send.at[owner], recv_sem=core_recv.at[owner],
            device_id=(me, mate), device_id_type=MESH,
        ).wait_recv()


def merge_kernel(
    width,
    slab, pair, gate, in_new, sq_new, ga_new, v_query, v_gate, v_out,
    m_query, m_gate, m_out, in_out, sq_out, ga_out,
    s_query, s_gate, s_out, state_sem, sem,
):
    n, rows = slab.shape[1], slab.shape[2]
    rank = n * rows

    states = [
        pltpu.make_async_copy(new, out, state_sem.at[i])
        for i, (new, out) in enumerate(((in_new, in_out), (sq_new, sq_out), (ga_new, ga_out)))
    ]
    for copy in states:
        copy.start()

    def flat(block):
        if rows % 16 == 0:
            return block.reshape(rank, block.shape[-1])
        return block.astype(F32).reshape(rank, block.shape[-1]).astype(BF16)

    def merge(which, held, staged, merged, left, rights, first, count):
        slots, tile = staged.shape[:2]
        done = first // tile

        def out_copy(i):
            slot = lax.rem(i, slots)
            at = pl.ds(pl.multiple_of(i * tile, tile), tile)
            return pltpu.make_async_copy(staged.at[slot], merged.at[at], sem.at[which, slot])

        def body(i, _):
            whole = done + i
            slot = lax.rem(whole, slots)

            @pl.when(whole >= slots)
            def _():
                out_copy(whole - slots).wait()

            at = pl.ds(pl.multiple_of(whole * tile, tile), tile)
            lhs = jnp.transpose(left(pl.ds(pl.multiple_of(i * tile, tile), tile)) * adapter_scale)
            for start, span, right in rights:
                step = 256
                for c in range(0, span, step):
                    change = jnp.dot(lhs, right(slice(c, c + step)), preferred_element_type=F32)
                    there = slice(start + c, start + c + step)
                    staged[slot, :, there] = (held[at, there].astype(F32) + change).astype(BF16)
            out_copy(whole).start()
            return 0

        lax.fori_loop(0, count // tile, body, 0)

    def drain(which, staged, merged):
        slots, tile = staged.shape[:2]
        steps = merged.shape[0] // tile
        for i in range(max(0, steps - slots), steps):
            pltpu.make_async_copy(
                staged.at[i % slots], merged.at[i * tile : (i + 1) * tile], sem.at[which, i % slots]
            ).wait()

    def slab_left(j, start):
        return lambda at: flat(slab[j, :, :, pl.ds(start + at.start, at.size)])

    hidden = gate.shape[2]
    for j in range(2):
        merge(
            0, v_gate, s_gate, m_gate, slab_left(j, width),
            ((0, hidden, lambda at: flat(gate[:, :, at])),), j * width, width,
        )
    for j in range(2):
        merge(
            1, v_query, s_query, m_query, slab_left(j, 0),
            ((0, width, lambda at: flat(pair[:, :, width + at.start : width + at.stop])),),
            j * width, width,
        )

    def out_right(j):
        return lambda at: flat(slab[j, :, :, 2 * width + at.start : 2 * width + at.stop])

    merge(
        2, v_out, s_out, m_out, lambda at: flat(pair[:, :, at]),
        ((0, width, out_right(0)), (width, width, out_right(1))), 0, width,
    )
    for which, (staged, merged) in enumerate(((s_gate, m_gate), (s_query, m_query), (s_out, m_out))):
        drain(which, staged, merged)
    for copy in states:
        copy.wait()


def on_device(
    n, lines,
    w_query, gate_weight, w_output, input_state, input_parts,
    square_state, square_parts, gate_state, gate_parts,
):
    in_state, in_parts = jnp.swapaxes(input_state, 2, 3), jnp.swapaxes(input_parts, 2, 3)
    rank, width = in_parts.shape[2:]
    rows = in_state.shape[2]
    hidden = gate_parts.shape[2]
    spans = (3 * width, 2 * width, hidden)
    dma = pltpu.SemaphoreType.DMA
    hbm = pl.BlockSpec(memory_space=pltpu.HBM)
    vmem = pl.BlockSpec(memory_space=pltpu.VMEM)

    held = pl.pallas_call(
        functools.partial(exchange_kernel, n, lines, width),
        out_shape=[
            pltpu.VMEM((2, n, rows, 3 * width), BF16),
            pltpu.VMEM((n, rows, 2 * width), BF16),
            pltpu.VMEM((n, rows, hidden), BF16),
            pltpu.VMEM(in_state.shape, F32),
            pltpu.VMEM(square_state.shape, F32),
            pltpu.VMEM(gate_state.shape, F32),
            pltpu.VMEM(w_query.shape, BF16),
            pltpu.VMEM(gate_weight.shape, BF16),
            pltpu.VMEM(w_output.shape, BF16),
        ],
        in_specs=[hbm] * 9,
        out_specs=[vmem] * 9,
        scratch_shapes=[
            pltpu.VMEM(in_parts.shape[1:], F32),
            pltpu.VMEM(square_parts.shape[1:], F32),
            pltpu.VMEM(gate_parts.shape[1:], F32),
            pltpu.VMEM(in_state.shape, F32),
            pltpu.VMEM(square_state.shape, F32),
            pltpu.VMEM(gate_state.shape, F32),
            *(pltpu.VMEM((n, rows, span), BF16) for span in spans),
            *(pltpu.VMEM((n - 1, rows, span), BF16) for span in spans),
            pltpu.VMEM((lines, rows, 3 * width), BF16),
            dma((6,)), dma((3,)), dma((3,)),
            dma((3, n - 1)), dma((3, n - 1)),
            dma((lines - 1,)), dma((lines - 1,)),
            dma((lines,)), dma((n,)),
            dma((n,)), dma((n,)),
            dma((2, n - 1)), dma((2, n - 1)),
        ],
        compiler_params=pltpu.CompilerParams(
            collective_id=0, has_side_effects=True, vmem_limit_bytes=16 * 2**20
        ),
        name="exchange",
    )(
        *(
            pltpu.with_memory_space_constraint(x, pltpu.HBM)
            for x in (
                in_parts, square_parts, gate_parts, in_state, square_state, gate_state,
                w_query, gate_weight, w_output,
            )
        )
    )
    merged_query, merged_gate, merged_output, new_input, new_square, new_gate = pl.pallas_call(
        functools.partial(merge_kernel, width),
        out_shape=[
            jax.ShapeDtypeStruct(w_query.shape, BF16),
            jax.ShapeDtypeStruct(gate_weight.shape, BF16),
            jax.ShapeDtypeStruct(w_output.shape, BF16),
            jax.ShapeDtypeStruct(in_state.shape, F32),
            jax.ShapeDtypeStruct(square_state.shape, F32),
            jax.ShapeDtypeStruct(gate_state.shape, F32),
        ],
        in_specs=[vmem] * 9,
        out_specs=[hbm] * 6,
        scratch_shapes=[
            *(pltpu.VMEM((3, 256, w.shape[1]), BF16) for w in (w_query, gate_weight, w_output)),
            dma((3,)),
            dma((3, 3)),
        ],
        compiler_params=pltpu.CompilerParams(vmem_limit_bytes=16 * 2**20),
        name="merge",
    )(*(pltpu.with_memory_space_constraint(x, pltpu.VMEM) for x in held))
    return (merged_query, merged_gate, merged_output, jnp.swapaxes(new_input, 2, 3), new_square, new_gate)


def solution(mesh):
    n, lines = mesh.shape["replica"], mesh.shape["rollout"] // 2
    assert n == lines
    return jax.shard_map(
        functools.partial(on_device, n, lines),
        mesh=mesh,
        in_specs=(
            P("replica", "rollout"),
            P("replica", "rollout"),
            P("rollout", "replica"),
            P(None, None, "rollout", "replica"),
            P("replica", None, "rollout", None),
            P(None, None, "replica", "rollout"),
            P("replica", None, None, "rollout"),
            P(None, "replica", "rollout"),
            P("replica", None, "rollout"),
        ),
        out_specs=(
            P("replica", "rollout"),
            P("replica", "rollout"),
            P("rollout", "replica"),
            P(None, None, "rollout", "replica"),
            P(None, None, "replica", "rollout"),
            P(None, "replica", "rollout"),
        ),
        check_vma=False,
    )
```
